128 devices in a mesh: sector: 16 (over z, x), mpo: 8 (over y, core).
Axes of the slice: x: 4, y: 4, z: 4, core: 2. Of those that a mesh axis runs over, the one named last changes fastest.
Arguments:
- psi: float32 [16, 768, 768], P('sector'), may hold values from -24 to 24, as said below
- left_env: float32 [8, 16, 768, 768], P('mpo', 'sector'), may hold values from -0.21875 to 0.21875
- right_env: float32 [8, 16, 768, 768], P('mpo', 'sector'), may hold values from -0.21875 to 0.21875
- sector_label: int32 [16], replicated, may hold values from 0 to 15, as said below
- charge_step: int32 [8, 16, 3], replicated, may hold values from -1 to 1
- coef_index: int32 [8, 16, 3], replicated, may hold values from 0 to 7
- entry_values: float32 [8], replicated, may hold values from -1.5 to 1.5
- recurrence: float32 [3], replicated, may hold values from -2 to 2
Outputs:
- vec_one: float32 [16, 768, 768], P('sector')
- vec_two: float32 [16, 768, 768], P('sector')
The draws below stay inside these ranges and needn't reach their ends.
Inputs may be any that keep to these rules, and one draw needn't show every extreme that they name: `psi`: each sector block's entries lie in this range. `sector_label`: A permutation of the labels over the slots; two sectors whose labels differ by one lie at most 3 slots apart.
All inputs are finite; a program needn't handle non-finite values.
Results may differ from the reference program's by a relative error of at most 0.0029.
Values may be sent and summed in bfloat16 or wider, within the bound.
No kernel may reach another device: no remote copies, remote signals or barrier semaphores. Data moves between devices by JAX's collectives and lax.ppermute only.
A program may use at most 64 MiB of HBM per device.

```python
import jax
import jax.numpy as jnp
from jax import lax

M = 768
K = 3
NCOEF = 8
SECTORS = 16
MPO_BOND = 8


def draw_psi(key, part):
    key_base, key_jitter = jax.random.split(key, 2)
    ramp_up = jnp.exp(jnp.log(3.0) * jnp.arange(SECTORS, dtype=jnp.float32) / (SECTORS - 1))
    jitter = jax.random.uniform(key_jitter, (SECTORS,), jnp.float32, 0.7, 1.3)
    base = jnp.clip(jax.random.normal(key_base, (SECTORS, M, M), jnp.float32), -6.0, 6.0)
    scales = ramp_up * jitter
    return base * scales[:, None, None]


def draw_sector_label(key, part):
    pair_count = SECTORS // 2
    swap_bits = jax.random.randint(jax.random.fold_in(key, 7), (pair_count,), 0, 2)
    forced = jax.random.randint(jax.random.fold_in(key, 11), (), 0, pair_count - 1)
    pair_ids = jnp.arange(pair_count, dtype=jnp.int32)
    swap_bits = jnp.where((pair_ids == forced) | (pair_ids == forced + 1), 1, swap_bits)
    mirror = jax.random.randint(jax.random.fold_in(key, 13), (), 0, 2)
    slots = jnp.arange(SECTORS, dtype=jnp.int32)
    per_slot = jnp.repeat(swap_bits, 2)
    labels = slots + per_slot * (1 - 2 * (slots % 2))
    labels = jnp.where(mirror == 1, SECTORS - 1 - labels, labels)
    return labels.astype(jnp.int32)


def plant(result, rng, smallest, largest):
    spot = [jax.random.randint(jax.random.fold_in(rng, axis), (), 0, length) for axis, length in enumerate(result.shape)]
    widest = result.shape.index(max(result.shape))
    neighbour = spot[:widest] + [(spot[widest] + 1) % result.shape[widest]] + spot[widest + 1:]
    return result.at[tuple(spot)].set(smallest).at[tuple(neighbour)].set(largest)


def block_scale(stream_key, dims, pieces, least, top_value):
    level, own = 1.0, jax.random.fold_in(stream_key, 6)
    for axis_at, parts in pieces:
        steps = jnp.exp(jax.random.uniform(jax.random.fold_in(own, axis_at), (parts,), jnp.float32, least / len(pieces), top_value / len(pieces)))
        level = level * jnp.repeat(steps, dims[axis_at] // parts).reshape([-1 if axis == axis_at else 1 for axis in range(len(dims))])
    return level


def scatter_about(rng, shape, scale, bound, cuts=(), kind=jnp.bfloat16):
    array = scale * jax.random.normal(rng, shape, jnp.float32)
    if cuts:
        array = array * block_scale(rng, shape, cuts, -0.22, 0.18)
    return jnp.clip(array, -bound, bound).astype(kind)


def setup_inputs(seed: int = 0) -> dict:
    splits = jax.random.split(jax.random.key(seed), 9)
    psi = draw_psi(jax.random.fold_in(splits[8], 71), 0)
    left_env = scatter_about(splits[1], (MPO_BOND, SECTORS, M, M), M ** -0.5, 0.21875, ((0, 8), (1, 16)), jnp.float32)
    right_env = scatter_about(splits[2], (MPO_BOND, SECTORS, M, M), M ** -0.5, 0.21875, ((0, 8), (1, 16)), jnp.float32)
    sector_label = draw_sector_label(jax.random.fold_in(splits[8], 71), 0)
    charge_step = plant(jax.random.randint(splits[4], (MPO_BOND, SECTORS, K), -1, 2), jax.random.fold_in(splits[4], 1), -1, 1).astype(jnp.int32)
    coef_index = plant(jax.random.randint(splits[5], (MPO_BOND, SECTORS, K), 0, NCOEF), jax.random.fold_in(splits[5], 1), 0, NCOEF - 1).astype(jnp.int32)
    entry_values = jnp.clip(jax.random.uniform(splits[6], (NCOEF,), jnp.float32, -1.5, 1.5), -1.5, 1.5)
    recurrence = jnp.clip(jax.random.uniform(splits[7], (3,), jnp.float32, -2.0, 2.0), -2.0, 2.0)
    return {"psi": psi, "left_env": left_env, "right_env": right_env, "sector_label": sector_label, "charge_step": charge_step, "coef_index": coef_index, "entry_values": entry_values, "recurrence": recurrence}


EPS = 1e-06
highest = lax.Precision.HIGHEST

def coupling_table(sector_label, charge_step, coef_index, entry_values):
    target = sector_label[None, :, None] + charge_step
    table = jnp.arange(entry_values.shape[0], dtype=jnp.int32)
    values = lax.optimization_barrier(jnp.sum(jnp.where(coef_index[..., None] == table, entry_values, jnp.float32(0.0)), axis=-1))
    matches = target[..., None] == sector_label[None, None, None, :]
    return lax.optimization_barrier(jnp.sum(jnp.where(matches, values[..., None], jnp.float32(0.0)), axis=2))

def apply_hamiltonian(vector, left_env, right_env, couple):

    def step_bond(summed, inputs):
        left_bond, right_bond, couple_bond = inputs
        product = jnp.einsum('sab,sbc->sac', left_bond, vector, precision=highest).astype(jnp.bfloat16)
        mixed = jnp.einsum('ji,jab->iab', couple_bond, product.astype(jnp.float32), precision=highest)
        return (summed + jnp.einsum('iab,ibc->iac', mixed, right_bond, precision=highest), None)
    summed, unused = lax.scan(step_bond, jnp.zeros(vector.shape, jnp.float32), (left_env, right_env, couple))
    return summed

def normalize(resid):
    return resid / jnp.sqrt(jnp.mean(resid * resid) + EPS)

def reference(psi, left_env, right_env, sector_label, charge_step, coef_index, entry_values, recurrence):
    couple = coupling_table(sector_label, charge_step, coef_index, entry_values)
    first = apply_hamiltonian(psi, left_env, right_env, couple)
    vec_one = normalize(first - recurrence[0] * psi)
    second = apply_hamiltonian(vec_one, left_env, right_env, couple)
    vec_two = normalize(second - recurrence[1] * vec_one - recurrence[2] * psi)
    return (vec_one, vec_two)
```

```python
import jax
import jax.numpy as jnp
from jax import lax
from jax.sharding import PartitionSpec as P

EPS = 1e-06
SIDE = 4
CHUNKS = 2
ENV = 0.21875
COUPLE = 13.5
F16_TOP = 60000.0
high = lax.Precision.HIGH


def along_x(block, step):
    route = [
        (SIDE * z + x, SIDE * z + (x + step) % SIDE) for z in range(SIDE) for x in range(SIDE)
    ]
    return lax.ppermute(block, "sector", route)


def along_z(block, step):
    count = SIDE * SIDE
    route = [
        (i, i + SIDE * step) for i in range(count) if 0 <= i + SIDE * step < count
    ]
    return lax.ppermute(block, "sector", route)


def around_z(block, step):
    count = SIDE * SIDE
    return lax.ppermute(
        block, "sector", [(i, (i + SIDE * step) % count) for i in range(count)]
    )


def along_y(block, step):
    route = [
        (2 * y + core, 2 * ((y + step) % SIDE) + core) for y in range(SIDE) for core in range(2)
    ]
    return lax.ppermute(block, "mpo", route)


def other_core(block):
    return lax.ppermute(block, "mpo", [(i, i ^ 1) for i in range(2 * SIDE)])


def pick(array, index):
    return lax.dynamic_index_in_dim(array, index, 0, keepdims=False)


def in_order(parts, position):
    ring = jnp.stack([parts[3], parts[2], parts[1], parts[0], parts[3], parts[2], parts[1]])
    return lax.dynamic_slice_in_dim(ring, SIDE - 1 - position, SIDE, 0)


def spread(pieces, position, move):
    return [pick(pieces, position)] + [
        move(pick(pieces, (position + d) % SIDE), d) for d in range(1, SIDE)
    ]


def local(
    psi, left_env, right_env, sector_label, charge_step, coef_index, entry_values, recurrence
):
    slot = lax.axis_index("sector")
    bond = lax.axis_index("mpo")
    z, x = slot // SIDE, slot % SIDE
    y, core = bond // 2, bond % 2
    psi, left, right = psi[0], left_env[0, 0], right_env[0, 0]
    m = psi.shape[0]
    slots = sector_label.shape[0]
    cells = float(slots * m * m)
    rows = m // CHUNKS
    part = rows // SIDE
    half = rows // 2
    eighth = half // SIDE

    table = jnp.arange(entry_values.shape[0], dtype=jnp.int32)
    every = jnp.arange(slots, dtype=jnp.int32)
    ds = jnp.arange(SIDE, dtype=jnp.int32)
    goal = SIDE * z + (x + ds) % SIDE
    source = jnp.concatenate(
        [
            SIDE * z + (x - ds) % SIDE,
            SIDE * (z - 1) + jnp.arange(1, SIDE, dtype=jnp.int32),
            SIDE * (z + 1) + jnp.arange(0, SIDE - 1, dtype=jnp.int32),
        ]
    )
    step_bond, index_bond = pick(charge_step, bond), pick(coef_index, bond)
    values = jnp.sum(
        jnp.where(index_bond[..., None] == table, entry_values, jnp.float32(0.0)), axis=-1
    )
    target = sector_label[:, None] + step_bond
    goal_label = jnp.sum(jnp.where(goal[:, None] == every, sector_label, 0), axis=1)
    into = jnp.sum(
        jnp.where(
            target[None] == goal_label[:, None, None], values[None], jnp.float32(0.0)
        ),
        axis=2,
    )
    weight = jnp.sum(
        jnp.where(source[None, :, None] == every, into[:, None, :], jnp.float32(0.0)), axis=2
    )

    def gather_numbers(numbers):
        tile = jnp.zeros((8, 128), jnp.float32).at[0, : numbers.shape[0]].set(numbers)
        line = jnp.stack([tile] + [along_x(tile, d) for d in range(1, SIDE)])
        grid = jnp.stack([line] + [around_z(line, d) for d in range(1, SIDE)])
        return grid[:, :, 0, : numbers.shape[0]]

    def exchange(pieces, row_scales, up_scales, down_scales, z_scale):
        near = spread(pieces, x, along_x)
        ordered = in_order(near, x)
        from_up = along_z(ordered[1:], 1)
        from_down = along_z(ordered[: SIDE - 1], -1)
        blocks = near + [from_up[i] for i in range(SIDE - 1)] + [from_down[i] for i in range(SIDE - 1)]
        if row_scales is None:
            blocks = [b.astype(jnp.float32) for b in blocks]
        else:
            scales = row_scales + up_scales + down_scales
            blocks = [
                (b.astype(jnp.float32) * s).astype(jnp.bfloat16).astype(jnp.float32)
                for b, s in zip(blocks, scales)
            ]
        sums = []
        for d in range(SIDE):
            total = weight[d, 0] * blocks[0]
            for j in range(1, len(blocks)):
                total = total + weight[d, j] * blocks[j]
            sums.append((total * z_scale).astype(jnp.float16))
        back = [sums[0]] + [along_x(sums[d], d) for d in range(1, SIDE)]
        return in_order(back, x).reshape(rows, m)

    def reduce_bonds(term, scale):
        halves = (term * scale).astype(jnp.float16).reshape(2, half, m)
        chip = pick(halves, core).astype(jnp.float32) + other_core(pick(halves, 1 - core)).astype(
            jnp.float32
        )
        quarters = chip.reshape(SIDE, eighth, m)
        got = spread(quarters.astype(jnp.float16), y, along_y)
        total = pick(quarters, y)
        for d in range(1, SIDE):
            total = total + got[d].astype(jnp.float32)
        return total

    def share_bonds(piece):
        mine = in_order([piece] + [along_y(piece, d) for d in range(1, SIDE)], y).reshape(half, m)
        theirs = other_core(mine)
        both = jnp.stack([theirs, mine, theirs])
        return lax.dynamic_slice_in_dim(both, 1 - core, 2, 0).reshape(rows, m)

    def own_rows(array, chunk):
        start = chunk * rows + core * half + y * eighth
        return lax.dynamic_slice_in_dim(array, start, eighth, 0)

    tiny = jnp.float32(1e-30)

    peak = jnp.max(gather_numbers(jnp.max(jnp.abs(psi))[None]))
    peak = jnp.maximum(peak, tiny)
    z_bound = peak * (m * ENV * COUPLE * 1.01)
    z_scale = F16_TOP / z_bound
    o_bound = z_bound * (2.02 * m * ENV)
    o_scale = F16_TOP / (4.0 * o_bound + 2.0 * peak)
    first = []
    for c in range(CHUNKS):
        product = jnp.dot(left[c * rows : (c + 1) * rows], psi, precision=high)
        pieces = product.astype(jnp.bfloat16).reshape(SIDE, part, m)
        mixed = exchange(pieces, None, None, None, z_scale).astype(jnp.float32) * (1.0 / z_scale)
        term = jnp.dot(mixed, right, precision=high)
        piece = reduce_bonds(term, o_scale)
        piece = piece - (o_scale * recurrence[0]) * own_rows(psi, c)
        first.append(share_bonds(piece.astype(jnp.float16)))
    resid = jnp.concatenate(first).astype(jnp.float32)

    numbers = gather_numbers(jnp.stack([jnp.sum(resid * resid), jnp.max(jnp.abs(resid))]))
    mean = jnp.sum(numbers[:, :, 0]) / cells
    gain = 1.0 / jnp.sqrt(mean + EPS * (o_scale * o_scale))
    vec_one = resid * gain

    peaks = jnp.maximum(numbers[:, :, 1], tiny)
    own_peak = jnp.maximum(jnp.max(jnp.abs(resid)), tiny)
    x_unit = m * ENV * 1.01 / F16_TOP
    row_scales = [peaks[0, e] * (x_unit * gain) for e in range(SIDE)]

    def scale_of(dz, xs):
        return pick(pick(peaks, dz % SIDE), (x - xs) % SIDE) * (x_unit * gain)

    up_scales = [scale_of(1, xs) for xs in range(1, SIDE)]
    down_scales = [scale_of(-1, xs) for xs in range(SIDE - 1)]
    peak_one = jnp.max(peaks) * gain
    z_bound = peak_one * (m * ENV * COUPLE * 1.01)
    z_scale = F16_TOP / z_bound
    o_bound = z_bound * (2.02 * m * ENV)
    o_scale2 = F16_TOP / (4.0 * o_bound + 2.0 * peak_one + 2.0 * peak)
    second = []
    for c in range(CHUNKS):
        product = jnp.dot(left[c * rows : (c + 1) * rows], resid, precision=high)
        pieces = (product * (1.0 / (x_unit * own_peak))).astype(jnp.float16)
        pieces = pieces.reshape(SIDE, part, m)
        mixed = exchange(pieces, row_scales, up_scales, down_scales, z_scale).astype(jnp.float32)
        term = jnp.dot(mixed * (1.0 / z_scale), right, precision=high)
        piece = reduce_bonds(term, o_scale2)
        piece = piece - (o_scale2 * recurrence[1]) * own_rows(vec_one, c)
        piece = piece - (o_scale2 * recurrence[2]) * own_rows(psi, c)
        second.append(share_bonds(piece.astype(jnp.float16)))
    resid = jnp.concatenate(second).astype(jnp.float32)
    numbers = gather_numbers(jnp.sum(resid * resid)[None])
    mean = jnp.sum(numbers) / cells
    vec_two = resid * (1.0 / jnp.sqrt(mean + EPS * (o_scale2 * o_scale2)))
    return (vec_one[None], vec_two[None])


def solution(mesh):
    in_specs = (
        P("sector", None, None),
        P("mpo", "sector", None, None),
        P("mpo", "sector", None, None),
        P(),
        P(),
        P(),
        P(),
        P(),
    )
    out_specs = (P("sector", None, None), P("sector", None, None))
    return jax.shard_map(local, mesh=mesh, in_specs=in_specs, out_specs=out_specs, check_vma=False)
```

```python
import functools

import jax
import jax.numpy as jnp
from jax import lax
from jax.experimental import pallas as pl
from jax.experimental.pallas import tpu as pltpu
from jax.sharding import PartitionSpec as P

EPS = 1e-06
SIDE = 4
CHUNKS = 2
ENV = 0.21875
COUPLE = 13.5
F16_TOP = 60000.0
F32, BF16, F16 = jnp.float32, jnp.bfloat16, jnp.float16
VMEM_LIMIT = 24 * 1024 * 1024
in_vmem = pl.BlockSpec(memory_space=pltpu.VMEM)
in_smem = pl.BlockSpec(memory_space=pltpu.SMEM)


def along_x(block, step):
    route = [
        (SIDE * z + x, SIDE * z + (x + step) % SIDE) for z in range(SIDE) for x in range(SIDE)
    ]
    return lax.ppermute(block, "sector", route)


def along_z(block, step):
    count = SIDE * SIDE
    route = [(i, i + SIDE * step) for i in range(count) if 0 <= i + SIDE * step < count]
    return lax.ppermute(block, "sector", route)


def around_z(block, step):
    count = SIDE * SIDE
    return lax.ppermute(
        block, "sector", [(i, (i + SIDE * step) % count) for i in range(count)]
    )


def along_y(block, step):
    route = [
        (2 * y + core, 2 * ((y + step) % SIDE) + core) for y in range(SIDE) for core in range(2)
    ]
    return lax.ppermute(block, "mpo", route)


def other_core(block):
    return lax.ppermute(block, "mpo", [(i, i ^ 1) for i in range(2 * SIDE)])


def pick(array, index):
    return lax.dynamic_index_in_dim(array, index, 0, keepdims=False)


def call(body, outs, smem, vmem, scratch=(), flops=0):
    shapes = [jax.ShapeDtypeStruct(shape, dtype) for shape, dtype in outs]
    moved = sum(a.size * a.dtype.itemsize for a in vmem)
    moved += sum(s.size * s.dtype.itemsize for s in shapes)
    return pl.pallas_call(
        body,
        out_shape=shapes,
        in_specs=[in_smem] * len(smem) + [in_vmem] * len(vmem),
        out_specs=[in_vmem] * len(outs),
        scratch_shapes=list(scratch),
        compiler_params=pltpu.CompilerParams(vmem_limit_bytes=VMEM_LIMIT),
        cost_estimate=pl.CostEstimate(flops=flops, bytes_accessed=moved, transcendentals=0),
    )(*smem, *vmem)


def halves_of(array):
    head = array.astype(BF16)
    return head, (array - head.astype(F32)).astype(BF16)


def dot(a, b):
    return jnp.dot(a, b, preferred_element_type=F32)


def split_kernel(rows, wide, head, tail, peak):
    def step(i, top):
        at = pl.ds(pl.multiple_of(i * rows, rows), rows)
        block = wide[at, :]
        head[at, :], tail[at, :] = halves_of(block)
        return jnp.maximum(top, jnp.max(jnp.abs(block).reshape(rows // 8, 8, -1), axis=0))

    top = lax.fori_loop(0, wide.shape[0] // rows, step, jnp.zeros((8, wide.shape[1]), F32))
    peak[...] = jnp.full(peak.shape, jnp.max(top), F32)


def product_kernel(row, place, scale, left, head, tail, *refs):
    outs, acc = refs[:SIDE], refs[SIDE]
    rows, part = acc.shape[0], acc.shape[0] // SIDE
    left_head, left_tail = halves_of(left[pl.ds(row, rows), :])
    wide = acc.shape[1] // 3
    for n in range(3):
        cols = slice(n * wide, (n + 1) * wide)
        h = head[:, cols]
        acc[:, cols] = dot(left_head, h) + (dot(left_head, tail[:, cols]) + dot(left_tail, h))
    x = place[0]
    factor = scale[0]
    for d in range(SIDE):
        start = pl.multiple_of(lax.rem(x + d, SIDE) * part, part)
        value = acc[pl.ds(start, part), :]
        if outs[d].dtype == F32:
            value = value * factor
        outs[d][...] = value.astype(outs[d].dtype)


def mix_kernel(rounded, weight, scale, *refs):
    singles, up, down, outs = refs[:SIDE], refs[SIDE], refs[SIDE + 1], refs[SIDE + 2 :]
    step_rows = 16

    def step(i, carry):
        at = pl.ds(pl.multiple_of(i * step_rows, step_rows), step_rows)
        blocks = [s[at, :] for s in singles]
        blocks += [up[j, at, :] for j in range(SIDE - 1)] + [down[j, at, :] for j in range(SIDE - 1)]
        sums = [None] * SIDE
        for j, block in enumerate(blocks):
            if rounded:
                block = (block * scale[j]).astype(BF16)
            block = block.astype(F32)
            for d in range(SIDE):
                term = block * weight[d * 10 + j]
                sums[d] = term if j == 0 else sums[d] + term
        for d in range(SIDE):
            outs[d][at, :] = sums[d]
        return carry

    lax.fori_loop(0, outs[0].shape[0] // step_rows, step, 0)


def term_kernel(place, scale, mixed, head, tail, mine, theirs, acc):
    eighth = mine.shape[1]
    half = SIDE * eighth
    left_head, left_tail = halves_of(mixed[...])
    wide = acc.shape[1] // 3
    for n in range(3):
        cols = slice(n * wide, (n + 1) * wide)
        h = head[:, cols]
        acc[:, cols] = dot(left_head, h) + (dot(left_head, tail[:, cols]) + dot(left_tail, h))
    y, core, factor = place[1], place[2], scale[0]
    for e in range(SIDE):
        quarter = lax.rem(y + e, SIDE) * eighth
        for out, side in ((mine, core), (theirs, 1 - core)):
            start = pl.multiple_of(side * half + quarter, eighth)
            out[e] = acc[pl.ds(start, eighth), :] * factor


def assemble_kernel(chunks, place, *refs):
    parts, outs, stats = refs[: 2 * chunks], refs[2 * chunks : -1], refs[-1]
    eighth = parts[0].shape[1]
    part = 2 * eighth
    x, y, core = place[0], place[1], place[2]
    m = parts[0].shape[2]
    squares, top = jnp.zeros((8, m), F32), jnp.zeros((8, m), F32)
    for c in range(chunks):
        for block, side in ((parts[2 * c], core), (parts[2 * c + 1], 1 - core)):
            for e in range(SIDE):
                quarter = lax.rem(y - e + SIDE, SIDE)
                d = 2 * side + quarter // 2
                k = lax.rem(x - d + SIDE, SIDE)
                start = c * SIDE * part + k * part + lax.rem(quarter, 2) * eighth
                at = pl.ds(pl.multiple_of(start, eighth), eighth)
                value = block[e]
                if len(outs) == 2:
                    outs[0][at, :], outs[1][at, :] = halves_of(value)
                else:
                    outs[0][at, :] = value
                tall = value.reshape(eighth // 8, 8, m)
                squares = squares + jnp.sum(tall * tall, axis=0)
                top = jnp.maximum(top, jnp.max(jnp.abs(tall), axis=0))
    lane = lax.broadcasted_iota(jnp.int32, stats.shape, 1)
    stats[...] = jnp.where(lane == 0, jnp.sum(squares), jnp.max(top))


def local(
    psi, left_env, right_env, sector_label, charge_step, coef_index, entry_values, recurrence
):
    slot = lax.axis_index("sector")
    bond = lax.axis_index("mpo")
    z, x = slot // SIDE, slot % SIDE
    y, core = bond // 2, bond % 2
    place = jnp.stack([x, y, core]).astype(jnp.int32)
    psi, left, right = psi[0], left_env[0, 0], right_env[0, 0]
    m = psi.shape[0]
    slots = sector_label.shape[0]
    cells = float(slots * m * m)
    rows = m // CHUNKS
    part = rows // SIDE
    half = rows // 2
    eighth = half // SIDE
    flops = 6 * rows * m * m

    ds = jnp.arange(SIDE, dtype=jnp.int32)
    three = ds[: SIDE - 1]
    skip_up, skip_down = x, (x + 1) % SIDE
    up_d = three + (three >= skip_up)
    down_d = three + (three >= skip_down)
    goal = SIDE * z + (x + ds) % SIDE
    source = jnp.concatenate(
        [
            SIDE * z + (x - ds) % SIDE,
            SIDE * (z - 1) + (x - up_d) % SIDE,
            SIDE * (z + 1) + (x - down_d) % SIDE,
        ]
    )
    relative = jnp.concatenate([ds, SIDE + up_d, 3 * SIDE + down_d])

    table = jnp.arange(entry_values.shape[0], dtype=jnp.int32)
    every = jnp.arange(slots, dtype=jnp.int32)
    step_bond, index_bond = pick(charge_step, bond), pick(coef_index, bond)
    values = jnp.sum(jnp.where(index_bond[..., None] == table, entry_values, F32(0.0)), axis=-1)
    target = sector_label[:, None] + step_bond
    goal_label = jnp.sum(jnp.where(goal[:, None] == every, sector_label, 0), axis=1)
    into = jnp.sum(
        jnp.where(target[None] == goal_label[:, None, None], values[None], F32(0.0)), axis=2
    )
    weight = jnp.sum(
        jnp.where(source[None, :, None] == every, into[:, None, :], F32(0.0)), axis=2
    ).reshape(-1)

    def gather_numbers(tile):
        line = jnp.stack([tile] + [along_x(tile, d) for d in range(1, SIDE)])
        grid = jnp.concatenate([line] + [around_z(line, d) for d in range(1, SIDE)])
        return grid

    def exchange(pieces, scales, weights):
        near = [pieces[0]] + [along_x(pieces[d], d) for d in range(1, SIDE)]
        up = jnp.stack([jnp.where(skip_up <= e, near[e + 1], near[e]) for e in range(SIDE - 1)])
        down = jnp.stack(
            [jnp.where(skip_down <= e, near[e + 1], near[e]) for e in range(SIDE - 1)]
        )
        blocks = near + [along_z(up, 1), along_z(down, -1)]
        rounded = scales is not None
        if rounded:
            blocks = [b.astype(F32) for b in blocks]
        else:
            scales = jnp.ones((10,), F32)
        sums = call(
            functools.partial(mix_kernel, rounded),
            [((part, m), F32)] * SIDE,
            [weights, scales],
            blocks,
            flops=80 * part * m,
        )
        sums = [s.astype(F16) for s in sums]
        return jnp.concatenate([sums[0]] + [along_x(sums[d], d) for d in range(1, SIDE)])

    def reduce_bonds(mixed, scale):
        mine, theirs = call(
            term_kernel,
            [((SIDE, eighth, m), F32)] * 2,
            [place, scale.reshape(1)],
            [mixed.astype(F32), right_head, right_tail],
            [pltpu.VMEM((rows, m), F32)],
            flops,
        )
        chip = mine + other_core(theirs.astype(F16)).astype(F32)
        sent = chip.astype(F16)
        total = chip[0]
        for e in range(1, SIDE):
            total = total + along_y(sent[e], e).astype(F32)
        return total

    def share_bonds(piece):
        mine = jnp.stack([piece] + [along_y(piece, e) for e in range(1, SIDE)])
        return [mine.astype(F32), other_core(mine).astype(F32)]

    def own_rows(array, chunk):
        k = (x - 2 * core - y // 2) % SIDE
        start = chunk * rows + k * part + (y % 2) * eighth
        return lax.dynamic_slice_in_dim(array, start, eighth, 0)

    def products(chunk, head, tail, dtype, scale):
        return call(
            functools.partial(product_kernel, chunk * rows),
            [((part, m), dtype)] * SIDE,
            [place, scale.reshape(1)],
            [left, head, tail],
            [pltpu.VMEM((rows, m), F32)],
            flops,
        )

    def split(array):
        square = ((m, m), BF16)
        return call(
            functools.partial(split_kernel, 32), [square, square, ((8, 128), F32)], [], [array]
        )

    def assemble(parts, outs):
        return call(
            functools.partial(assemble_kernel, CHUNKS), outs + [((8, 128), F32)], [place], parts
        )

    tiny = F32(1e-30)
    one = F32(1.0)

    head, tail, peak = split(psi)
    pieces = [products(c, head, tail, BF16, one) for c in range(CHUNKS)]
    right_head, right_tail, _ = split(right)
    peak = jnp.maximum(jnp.max(gather_numbers(peak)), tiny)
    z_bound = peak * (m * ENV * COUPLE * 1.01)
    z_scale = F16_TOP / z_bound
    o_bound = z_bound * (2.02 * m * ENV)
    o_scale = F16_TOP / (4.0 * o_bound + 2.0 * peak)
    mixed = [exchange(p, None, weight * z_scale) for p in pieces]
    parts = []
    for c in range(CHUNKS):
        piece = reduce_bonds(mixed[c], o_scale / z_scale)
        piece = piece - (o_scale * recurrence[0]) * own_rows(psi, c)
        parts += share_bonds(piece.astype(F16))
    square = ((m, m), BF16)
    head, tail, stats = assemble(parts, [square, square])

    x_unit = m * ENV * 1.01 / F16_TOP
    own_peak = jnp.maximum(stats[0, 1], tiny)
    pieces = [products(c, head, tail, F32, 1.0 / (x_unit * own_peak)) for c in range(CHUNKS)]
    numbers = gather_numbers(stats)
    mean = jnp.sum(numbers[:, 0, 0]) / cells
    gain = 1.0 / jnp.sqrt(mean + EPS * (o_scale * o_scale))
    peaks = jnp.maximum(numbers[:, 0, 1], tiny)
    scales = jnp.sum(
        jnp.where(relative[:, None] == every, peaks * (x_unit * gain), F32(0.0)), axis=1
    )
    peak_one = jnp.max(peaks) * gain
    z_bound = peak_one * (m * ENV * COUPLE * 1.01)
    z_scale = F16_TOP / z_bound
    o_bound = z_bound * (2.02 * m * ENV)
    o_scale = F16_TOP / (4.0 * o_bound + 2.0 * peak_one + 2.0 * peak)
    mixed = [exchange([a.astype(F16) for a in p], scales, weight * z_scale) for p in pieces]
    vec_one = (head.astype(F32) + tail.astype(F32)) * gain
    parts = []
    for c in range(CHUNKS):
        piece = reduce_bonds(mixed[c], o_scale / z_scale)
        piece = piece - (o_scale * recurrence[1]) * own_rows(vec_one, c)
        piece = piece - (o_scale * recurrence[2]) * own_rows(psi, c)
        parts += share_bonds(piece.astype(F16))
    resid, stats = assemble(parts, [((m, m), F32)])
    mean = jnp.sum(gather_numbers(stats)[:, 0, 0]) / cells
    vec_two = resid * (1.0 / jnp.sqrt(mean + EPS * (o_scale * o_scale)))
    return (vec_one[None], vec_two[None])


def solution(mesh):
    in_specs = (
        P("sector", None, None),
        P("mpo", "sector", None, None),
        P("mpo", "sector", None, None),
        P(),
        P(),
        P(),
        P(),
        P(),
    )
    out_specs = (P("sector", None, None), P("sector", None, None))
    return jax.shard_map(local, mesh=mesh, in_specs=in_specs, out_specs=out_specs, check_vma=False)
```

```python
import functools

import jax
import jax.numpy as jnp
from jax import lax
from jax.experimental import pallas as pl
from jax.experimental.pallas import tpu as pltpu
from jax.sharding import PartitionSpec as P

EPS = 1e-06
SIDE = 4
CHUNKS = 2
ENV = 0.21875
F16_TOP = 60000.0
F32, BF16, F16 = jnp.float32, jnp.bfloat16, jnp.float16
VMEM_LIMIT = 16 * 1024 * 1024
in_vmem = pl.BlockSpec(memory_space=pltpu.VMEM)
in_smem = pl.BlockSpec(memory_space=pltpu.SMEM)


def along_x(block, step):
    route = [
        (SIDE * z + x, SIDE * z + (x + step) % SIDE) for z in range(SIDE) for x in range(SIDE)
    ]
    return lax.ppermute(block, "sector", route)


def along_z(block, step):
    count = SIDE * SIDE
    route = [(i, i + SIDE * step) for i in range(count) if 0 <= i + SIDE * step < count]
    return lax.ppermute(block, "sector", route)


def around_z(block, step):
    count = SIDE * SIDE
    return lax.ppermute(
        block, "sector", [(i, (i + SIDE * step) % count) for i in range(count)]
    )


def along_y(block, step):
    route = [
        (2 * y + core, 2 * ((y + step) % SIDE) + core) for y in range(SIDE) for core in range(2)
    ]
    return lax.ppermute(block, "mpo", route)


def other_core(block):
    return lax.ppermute(block, "mpo", [(i, i ^ 1) for i in range(2 * SIDE)])


def pick(array, index):
    return lax.dynamic_index_in_dim(array, index, 0, keepdims=False)


def call(body, outs, smem, vmem, scratch=(), flops=0):
    shapes = [jax.ShapeDtypeStruct(shape, dtype) for shape, dtype in outs]
    moved = sum(a.size * a.dtype.itemsize for a in vmem)
    moved += sum(s.size * s.dtype.itemsize for s in shapes)
    return pl.pallas_call(
        body,
        out_shape=shapes,
        in_specs=[in_smem] * len(smem) + [in_vmem] * len(vmem),
        out_specs=[in_vmem] * len(outs),
        scratch_shapes=list(scratch),
        compiler_params=pltpu.CompilerParams(vmem_limit_bytes=VMEM_LIMIT),
        cost_estimate=pl.CostEstimate(flops=flops, bytes_accessed=moved, transcendentals=0),
    )(*smem, *vmem)


def halves_of(array):
    head = array.astype(BF16)
    return head, (array - head.astype(F32)).astype(BF16)


def dot(a, b):
    return jnp.dot(a, b, preferred_element_type=F32)


def product_kernel(row, place, scale, left, vector, *refs):
    outs, acc, stats = refs[:SIDE], refs[-1], refs[SIDE:-1]
    rows, m = acc.shape
    part = rows // SIDE
    left_head, left_tail = halves_of(left[pl.ds(row, rows), :])
    wide = m // 3
    squares = jnp.zeros((8, wide), F32)
    for n in range(3):
        cols = slice(n * wide, (n + 1) * wide)
        value = vector[:, cols]
        if stats:
            squares = squares + jnp.sum((value * value).reshape(-1, 8, wide), axis=0)
        head, tail = halves_of(value)
        acc[:, cols] = dot(left_head, head) + (dot(left_head, tail) + dot(left_tail, head))
    if stats:
        stats[0][...] = jnp.full(stats[0].shape, jnp.sum(squares), F32)
    x = place[0]
    factor = scale[0]
    for d in range(SIDE):
        start = pl.multiple_of(lax.rem(x + d, SIDE) * part, part)
        value = acc[pl.ds(start, part), :]
        if outs[d].dtype == F32:
            value = value * factor
        outs[d][...] = value.astype(outs[d].dtype)


def mix_kernel(rounded, weight, scale, near, up, down, out):
    step_rows = 16

    def step(i, carry):
        at = pl.ds(pl.multiple_of(i * step_rows, step_rows), step_rows)
        blocks = [near[j, at, :] for j in range(SIDE)]
        blocks += [up[j, at, :] for j in range(SIDE - 1)] + [down[j, at, :] for j in range(SIDE - 1)]
        sums = [None] * SIDE
        for j, block in enumerate(blocks):
            if rounded:
                block = (block * scale[0]).astype(BF16)
            block = block.astype(F32)
            for d in range(SIDE):
                term = block * weight[d * 10 + j]
                sums[d] = term if j == 0 else sums[d] + term
        for d in range(SIDE):
            out[d, at, :] = sums[d]
        return carry

    lax.fori_loop(0, out.shape[1] // step_rows, step, 0)


def term_kernel(place, scale, mixed, right, mine, theirs, acc):
    eighth = mine.shape[1]
    half = SIDE * eighth
    left_head, left_tail = halves_of(mixed[...])
    wide = acc.shape[1] // 3
    for n in range(3):
        cols = slice(n * wide, (n + 1) * wide)
        head, tail = halves_of(right[:, cols])
        acc[:, cols] = dot(left_head, head) + (dot(left_head, tail) + dot(left_tail, head))
    y, core, factor = place[1], place[2], scale[0]
    for e in range(SIDE):
        quarter = lax.rem(y + e, SIDE) * eighth
        for out, side in ((mine, core), (theirs, 1 - core)):
            start = pl.multiple_of(side * half + quarter, eighth)
            out[e] = acc[pl.ds(start, eighth), :] * factor


def assemble_kernel(place, mine, theirs, out, stats):
    chunks, eighth, m = mine.shape[1:]
    part = 2 * eighth
    x, y, core = place[0], place[1], place[2]
    squares = jnp.zeros((8, m), F32)
    for c in range(chunks):
        for block, side in ((mine, core), (theirs, 1 - core)):
            for e in range(SIDE):
                quarter = lax.rem(y - e + SIDE, SIDE)
                k = lax.rem(x - 2 * side - quarter // 2 + SIDE, SIDE)
                start = c * SIDE * part + k * part + lax.rem(quarter, 2) * eighth
                value = block[e, c]
                out[pl.ds(pl.multiple_of(start, eighth), eighth), :] = value
                squares = squares + jnp.sum((value * value).reshape(-1, 8, m), axis=0)
    stats[...] = jnp.full(stats.shape, jnp.sum(squares), F32)


def combined(tiles):
    row = lax.broadcasted_iota(jnp.int32, tiles[0].shape, 0)
    total = functools.reduce(jnp.add, tiles)
    return jnp.where(row == 0, total, functools.reduce(jnp.maximum, tiles))


def of_all_sectors(tile):
    line = combined([tile] + [along_x(tile, d) for d in range(1, SIDE)])
    return combined([line] + [around_z(line, d) for d in range(1, SIDE)])


def local(
    psi, left_env, right_env, sector_label, charge_step, coef_index, entry_values, recurrence
):
    slot = lax.axis_index("sector")
    bond = lax.axis_index("mpo")
    z, x = slot // SIDE, slot % SIDE
    y, core = bond // 2, bond % 2
    place = jnp.stack([x, y, core]).astype(jnp.int32)
    psi, left, right = psi[0], left_env[0, 0], right_env[0, 0]
    m = psi.shape[0]
    slots = sector_label.shape[0]
    cells = float(slots * m * m)
    rows = m // CHUNKS
    part = rows // SIDE
    half = rows // 2
    eighth = half // SIDE
    flops = 6 * rows * m * m

    ds = jnp.arange(SIDE, dtype=jnp.int32)
    three = ds[: SIDE - 1]
    skip_up, skip_down = x, (x + 1) % SIDE
    up_d = three + (three >= skip_up)
    down_d = three + (three >= skip_down)
    goal = SIDE * z + (x + ds) % SIDE
    source = jnp.concatenate(
        [
            SIDE * z + (x - ds) % SIDE,
            SIDE * (z - 1) + (x - up_d) % SIDE,
            SIDE * (z + 1) + (x - down_d) % SIDE,
        ]
    )

    table = jnp.arange(entry_values.shape[0], dtype=jnp.int32)
    every = jnp.arange(slots, dtype=jnp.int32)
    step_bond, index_bond = pick(charge_step, bond), pick(coef_index, bond)
    values = jnp.sum(jnp.where(index_bond[..., None] == table, entry_values, F32(0.0)), axis=-1)
    target = sector_label[:, None] + step_bond
    goal_label = jnp.sum(jnp.where(goal[:, None] == every, sector_label, 0), axis=1)
    into = jnp.sum(
        jnp.where(target[None] == goal_label[:, None, None], values[None], F32(0.0)), axis=2
    )
    weight = jnp.sum(
        jnp.where(source[None, :, None] == every, into[:, None, :], F32(0.0)), axis=2
    ).reshape(-1)

    def exchange(pieces, unit, weights):
        near = [pieces[0]] + [along_x(pieces[d], d) for d in range(1, SIDE)]
        up = jnp.stack([jnp.where(skip_up <= e, near[e + 1], near[e]) for e in range(SIDE - 1)])
        down = jnp.stack(
            [jnp.where(skip_down <= e, near[e + 1], near[e]) for e in range(SIDE - 1)]
        )
        blocks = [jnp.stack(near), along_z(up, 1), along_z(down, -1)]
        rounded = unit is not None
        if rounded:
            blocks = [b.astype(F32) for b in blocks]
        else:
            unit = one
        sums = call(
            functools.partial(mix_kernel, rounded),
            [((SIDE, part, m), F32)],
            [weights, unit.reshape(1)],
            blocks,
            flops=80 * part * m,
        )[0].astype(F16)
        return jnp.concatenate([sums[0]] + [along_x(sums[d], d) for d in range(1, SIDE)])

    def reduce_bonds(mixed, scale):
        chips = []
        for c in range(CHUNKS):
            mine, theirs = call(
                term_kernel,
                [((SIDE, eighth, m), F32)] * 2,
                [place, scale.reshape(1)],
                [mixed[c].astype(F32), right],
                [pltpu.VMEM((rows, m), F32)],
                flops,
            )
            chips.append(mine + other_core(theirs.astype(F16)).astype(F32))
        chip = jnp.stack(chips, 1)
        sent = chip.astype(F16)
        total = chip[0]
        for e in range(1, SIDE):
            total = total + along_y(sent[e], e).astype(F32)
        return total

    def share_bonds(piece):
        mine = jnp.stack([piece] + [along_y(piece, e) for e in range(1, SIDE)])
        return call(
            assemble_kernel,
            [((m, m), F32), ((8, 128), F32)],
            [place],
            [mine.astype(F32), other_core(mine).astype(F32)],
        )

    def own_rows(array):
        k = (x - 2 * core - y // 2) % SIDE
        start = k * part + (y % 2) * eighth
        return lax.dynamic_slice_in_dim(array.reshape(CHUNKS, rows, m), start, eighth, 1)

    def products(chunk, vector, dtype, scale, stats=False):
        return call(
            functools.partial(product_kernel, chunk * rows),
            [((part, m), dtype)] * SIDE + [((8, 128), F32)] * stats,
            [place, scale.reshape(1)],
            [left, vector],
            [pltpu.VMEM((rows, m), F32)],
            flops,
        )

    tiny = F32(1e-30)
    one = F32(1.0)
    reach = ENV * m**0.5
    spread_of = 9.0 * jnp.max(jnp.abs(entry_values)) + tiny

    *pieces, tile = products(0, psi, BF16, one, True)
    pieces = [pieces] + [products(c, psi, BF16, one) for c in range(1, CHUNKS)]
    tile = lax.optimization_barrier((tile, pieces[-1][0]))[0]
    top = jnp.sqrt(of_all_sectors(tile)[1, 0]) + tiny
    z_scale = F16_TOP / (1.02 * reach * spread_of * top)
    o_scale = F16_TOP / ((8.4 * reach * reach * spread_of + 2.1) * top)
    mixed = [exchange(p, None, weight * z_scale) for p in pieces]
    piece = reduce_bonds(mixed, o_scale / z_scale)
    piece = piece - (o_scale * recurrence[0]) * own_rows(psi)
    resid, tile = share_bonds(piece.astype(F16))

    x_unit = 1.01 * ENV * m
    inverse = F32(1.0 / x_unit)
    pieces = [products(c, resid, F32, inverse) for c in range(CHUNKS)]
    pieces = [[a.astype(F16) for a in p] for p in pieces]
    tile = lax.optimization_barrier((tile, pieces[-1][0]))[0]
    tile = of_all_sectors(tile)
    gain = 1.0 / jnp.sqrt(tile[0, 0] / cells + EPS * (o_scale * o_scale))
    top_one = jnp.sqrt(tile[1, 0]) * gain + tiny
    z_scale = F16_TOP / (1.02 * reach * spread_of * top_one)
    o_scale = F16_TOP / ((8.4 * reach * reach * spread_of + 2.1) * top_one + 2.1 * top)
    mixed = [exchange(p, x_unit * gain, weight * z_scale) for p in pieces]
    vec_one = resid * gain
    piece = reduce_bonds(mixed, o_scale / z_scale)
    piece = piece - (o_scale * recurrence[1]) * own_rows(vec_one)
    piece = piece - (o_scale * recurrence[2]) * own_rows(psi)
    resid, tile = share_bonds(piece.astype(F16))
    mean = of_all_sectors(tile)[0, 0] / cells
    vec_two = resid * (1.0 / jnp.sqrt(mean + EPS * (o_scale * o_scale)))
    return (vec_one[None], vec_two[None])


def solution(mesh):
    in_specs = (
        P("sector", None, None),
        P("mpo", "sector", None, None),
        P("mpo", "sector", None, None),
        P(),
        P(),
        P(),
        P(),
        P(),
    )
    out_specs = (P("sector", None, None), P("sector", None, None))
    return jax.shard_map(local, mesh=mesh, in_specs=in_specs, out_specs=out_specs, check_vma=False)
```

```python
import functools

import jax
import jax.numpy as jnp
from jax import lax
from jax.experimental import pallas as pl
from jax.experimental.pallas import tpu as pltpu
from jax.sharding import PartitionSpec as P

EPS = 1e-06
SIDE = 4
CHUNKS = 2
LATE = True
WHEN = 1
ENV = 0.21875
F16_TOP = 60000.0
TILE = 16
NOTE = 130.0
F32, BF16, F16 = jnp.float32, jnp.bfloat16, jnp.float16
VMEM_LIMIT = 16 * 1024 * 1024
in_vmem = pl.BlockSpec(memory_space=pltpu.VMEM)
in_smem = pl.BlockSpec(memory_space=pltpu.SMEM)


def along_x(block, step):
    route = [
        (SIDE * z + x, SIDE * z + (x + step) % SIDE) for z in range(SIDE) for x in range(SIDE)
    ]
    return lax.ppermute(block, "sector", route)


def along_z(block, step):
    count = SIDE * SIDE
    route = [(i, i + SIDE * step) for i in range(count) if 0 <= i + SIDE * step < count]
    return lax.ppermute(block, "sector", route)


def around_z(block, step):
    count = SIDE * SIDE
    return lax.ppermute(
        block, "sector", [(i, (i + SIDE * step) % count) for i in range(count)]
    )


def along_y(block, step):
    route = [
        (2 * y + core, 2 * ((y + step) % SIDE) + core) for y in range(SIDE) for core in range(2)
    ]
    return lax.ppermute(block, "mpo", route)


def other_core(block):
    return lax.ppermute(block, "mpo", [(i, i ^ 1) for i in range(2 * SIDE)])


def pick(array, index):
    return lax.dynamic_index_in_dim(array, index, 0, keepdims=False)


def after(value, earlier):
    return lax.optimization_barrier((value, earlier))[0]


def call(body, outs, smem, vmem, scratch=(), flops=0):
    shapes = [jax.ShapeDtypeStruct(shape, dtype) for shape, dtype in outs]
    moved = sum(a.size * a.dtype.itemsize for a in vmem)
    moved += sum(s.size * s.dtype.itemsize for s in shapes)
    return pl.pallas_call(
        body,
        out_shape=shapes,
        in_specs=[in_smem] * len(smem) + [in_vmem] * len(vmem),
        out_specs=[in_vmem] * len(outs),
        scratch_shapes=list(scratch),
        compiler_params=pltpu.CompilerParams(vmem_limit_bytes=VMEM_LIMIT),
        cost_estimate=pl.CostEstimate(flops=flops, bytes_accessed=moved, transcendentals=0),
    )(*smem, *vmem)


def halves_of(array):
    head = array.astype(BF16)
    return head, (array - head.astype(F32)).astype(BF16)


def dot(a, b):
    return jnp.dot(a, b, preferred_element_type=F32)


def product_kernel(row, noted, place, left, vector, squares, *refs):
    outs, acc = refs[:SIDE], refs[-1]
    rows, m = acc.shape
    part = rows // SIDE
    left_head, left_tail = halves_of(left[pl.ds(row, rows), :])
    wide = m // 3
    for n in range(3):
        cols = slice(n * wide, (n + 1) * wide)
        head, tail = halves_of(vector[:, cols])
        acc[:, cols] = dot(left_head, head) + (dot(left_head, tail) + dot(left_tail, head))
    x = place[0]
    if noted:
        power = jnp.ceil(0.5 * jnp.log2(jnp.clip(squares[...], 1e-36, 1e36)) + 0.01)
        note = jnp.broadcast_to(power[:1, :1] + NOTE, (TILE, m)).astype(BF16)
    for d in range(SIDE):
        start = pl.multiple_of(lax.rem(x + d, SIDE) * part, part)
        outs[d][:part, :] = acc[pl.ds(start, part), :].astype(BF16)
        if noted:
            outs[d][part:, :] = note


def squares_kernel(vector, out):
    rows, m = vector.shape
    step_rows = 64

    def step(i, total):
        value = vector[pl.ds(pl.multiple_of(i * step_rows, step_rows), step_rows), :]
        return total + jnp.sum((value * value).reshape(-1, 8, m), axis=0)

    total = lax.fori_loop(0, rows // step_rows, step, jnp.zeros((8, m), F32))
    out[...] = jnp.full(out.shape, jnp.sum(total), F32)


def select_kernel(part, skips, *refs):
    near, outs = refs[:SIDE], refs[SIDE:]
    for skip, out in ((skips[0], outs[0]), (skips[1], outs[1])):
        for e in range(SIDE):
            at = jnp.where(skip < e, e - 1, min(e, SIDE - 2)) * part

            @pl.when(skip != e)
            def _():
                out[pl.ds(pl.multiple_of(at, part), part), :] = near[e][:part, :]

        if near[0].shape[0] > part:
            notes = [n[part:, :].astype(F32) for n in near]
            out[(SIDE - 1) * part :, :] = functools.reduce(jnp.maximum, notes).astype(BF16)


def mix_kernel(noted, weight, scale, *refs):
    near, up, down = refs[:SIDE], refs[SIDE], refs[SIDE + 1]
    if noted:
        out, note = refs[SIDE + 2 :]
        part = out.shape[1]
        notes = [n[part:, :].astype(F32) for n in near]
        notes += [n[(SIDE - 1) * part :, :].astype(F32) for n in (up, down)]
        note[...] = functools.reduce(jnp.maximum, notes)
    else:
        note, out = refs[SIDE + 2 :]
        part = out.shape[1]
    factor = jnp.exp2(NOTE - note[...]) * scale[0]

    def step(i, carry):
        def at(piece):
            return pl.ds(pl.multiple_of(piece * part + i * TILE, TILE), TILE)

        blocks = [near[j][at(0), :] for j in range(SIDE)]
        blocks += [up[at(j), :] for j in range(SIDE - 1)] + [down[at(j), :] for j in range(SIDE - 1)]
        sums = [None] * SIDE
        for j, block in enumerate(blocks):
            block = block.astype(F32)
            for d in range(SIDE):
                term = block * weight[d * 10 + j]
                sums[d] = term if j == 0 else sums[d] + term
        for d in range(SIDE):
            out[d, at(0), :] = sums[d] * factor
        return carry

    lax.fori_loop(0, part // TILE, step, 0)


def term_kernel(place, scale, mixed, right, mine, theirs, acc):
    eighth = mine.shape[1]
    half = SIDE * eighth
    left_head, left_tail = halves_of(mixed[...])
    wide = acc.shape[1] // 3
    for n in range(3):
        cols = slice(n * wide, (n + 1) * wide)
        head, tail = halves_of(right[:, cols])
        acc[:, cols] = dot(left_head, head) + (dot(left_head, tail) + dot(left_tail, head))
    y, core, factor = place[1], place[2], scale[0]
    for e in range(SIDE):
        quarter = lax.rem(y + e, SIDE) * eighth
        for out, side in ((mine, core), (theirs, 1 - core)):
            start = pl.multiple_of(side * half + quarter, eighth)
            out[e] = acc[pl.ds(start, eighth), :] * factor


def assemble_kernel(place, scale, mine, theirs, out, stats):
    chunks, eighth, m = mine.shape[1:]
    part = 2 * eighth
    x, y, core = place[0], place[1], place[2]
    squares = jnp.zeros((8, m), F32)
    for c in range(chunks):
        for block, side in ((mine, core), (theirs, 1 - core)):
            for e in range(SIDE):
                quarter = lax.rem(y - e + SIDE, SIDE)
                k = lax.rem(x - 2 * side - quarter // 2 + SIDE, SIDE)
                start = c * SIDE * part + k * part + lax.rem(quarter, 2) * eighth
                value = block[e, c] * scale[0]
                out[pl.ds(pl.multiple_of(start, eighth), eighth), :] = value
                squares = squares + jnp.sum((value * value).reshape(-1, 8, m), axis=0)
    stats[...] = jnp.full(stats.shape, jnp.sum(squares), F32)


def combined(tiles):
    return functools.reduce(jnp.add, tiles)


def of_line(tile):
    return combined([tile] + [along_x(tile, d) for d in range(1, SIDE)])


def of_lines(line):
    return combined([line] + [around_z(line, d) for d in range(1, SIDE)])


def local(
    psi, left_env, right_env, sector_label, charge_step, coef_index, entry_values, recurrence
):
    slot = lax.axis_index("sector")
    bond = lax.axis_index("mpo")
    z, x = slot // SIDE, slot % SIDE
    y, core = bond // 2, bond % 2
    place = jnp.stack([x, y, core]).astype(jnp.int32)
    psi, left, right = psi[0], left_env[0, 0], right_env[0, 0]
    m = psi.shape[0]
    slots = sector_label.shape[0]
    cells = float(slots * m * m)
    rows = m // CHUNKS
    part = rows // SIDE
    half = rows // 2
    eighth = half // SIDE
    flops = 6 * rows * m * m

    ds = jnp.arange(SIDE, dtype=jnp.int32)
    three = ds[: SIDE - 1]
    skip_up, skip_down = x, (x + 1) % SIDE
    skips = jnp.stack([skip_up, skip_down]).astype(jnp.int32)
    up_d = three + (three >= skip_up)
    down_d = three + (three >= skip_down)
    goal = SIDE * z + (x + ds) % SIDE
    source = jnp.concatenate(
        [
            SIDE * z + (x - ds) % SIDE,
            SIDE * (z - 1) + (x - up_d) % SIDE,
            SIDE * (z + 1) + (x - down_d) % SIDE,
        ]
    )

    table = jnp.arange(entry_values.shape[0], dtype=jnp.int32)
    every = jnp.arange(slots, dtype=jnp.int32)
    step_bond, index_bond = pick(charge_step, bond), pick(coef_index, bond)
    values = jnp.sum(jnp.where(index_bond[..., None] == table, entry_values, F32(0.0)), axis=-1)
    target = sector_label[:, None] + step_bond
    goal_label = jnp.sum(jnp.where(goal[:, None] == every, sector_label, 0), axis=1)
    into = jnp.sum(
        jnp.where(target[None] == goal_label[:, None, None], values[None], F32(0.0)), axis=2
    )
    weight = jnp.sum(
        jnp.where(source[None, :, None] == every, into[:, None, :], F32(0.0)), axis=2
    ).reshape(-1)

    def spread(pieces):
        return [pieces[0]] + [along_x(pieces[d], d) for d in range(1, SIDE)]

    def next_rows(near, earlier):
        noted = near[0].shape[0] > part
        out = (((SIDE - 1) * part + TILE * noted, m), BF16)
        up, down = call(functools.partial(select_kernel, part), [out] * 2, [skips], near)
        up, down = after((up, down), earlier)
        return [along_z(up, 1), along_z(down, -1)]

    def mix(near, beyond, note, weights):
        noted = near[0].shape[0] > part
        out, note_out = ((SIDE, part, m), F32), ((TILE, m), F32)
        got = call(
            functools.partial(mix_kernel, noted),
            [out] + [note_out] * noted,
            [weights, z_scale.reshape(1)],
            near + beyond + ([] if noted else [note]),
            flops=80 * part * m,
        )
        sums = got[0].astype(F16)
        mixed = jnp.concatenate([sums[0]] + [along_x(sums[d], d) for d in range(1, SIDE)])
        return mixed, got[1] if noted else note

    def reduce_bonds(mixed, scale):
        chips = []
        for c in range(CHUNKS):
            mine, theirs = call(
                term_kernel,
                [((SIDE, eighth, m), F32)] * 2,
                [place, scale.reshape(1)],
                [mixed[c].astype(F32), right],
                [pltpu.VMEM((rows, m), F32)],
                flops,
            )
            chips.append(mine + other_core(theirs.astype(F16)).astype(F32))
        chip = jnp.stack(chips, 1)
        sent = chip.astype(F16)
        total = chip[0]
        for e in range(1, SIDE):
            total = total + along_y(sent[e], e).astype(F32)
        return total

    def share_bonds(piece, factor):
        mine = jnp.stack([piece] + [along_y(piece, e) for e in range(1, SIDE)])
        return call(
            assemble_kernel,
            [((m, m), F32), ((8, 128), F32)],
            [place, factor.reshape(1)],
            [mine.astype(F32), other_core(mine).astype(F32)],
        )

    def own_rows(array):
        k = (x - 2 * core - y // 2) % SIDE
        start = k * part + (y % 2) * eighth
        return lax.dynamic_slice_in_dim(array.reshape(CHUNKS, rows, m), start, eighth, 1)

    def products(chunk, vector, squares):
        noted = chunk == 0
        return call(
            functools.partial(product_kernel, chunk * rows, noted),
            [((part + TILE * noted, m), BF16)] * SIDE,
            [place],
            [left, vector, squares],
            [pltpu.VMEM((rows, m), F32)],
            flops,
        )

    def hamiltonian(vector, squares, summed):
        pieces = [products(c, vector, squares) for c in range(CHUNKS)]
        near, beyond, mixed, note, total = [], [], [], None, squares
        for p in pieces:
            near.append(after(spread(after(p, near[-1:])), pieces[-1][0]))
        scaled = weight
        if summed:
            line = of_line(after(squares, pieces[-1][0]))
            if LATE:
                near[-1] = after(near[-1], line)
        for p in near:
            beyond.append(next_rows(p, beyond[-1:]))
        if summed:
            total = of_lines(line)
        for c in range(CHUNKS):
            if summed and c == WHEN:
                scaled = after(scaled, total)
            rows_mixed, note = mix(near[c], beyond[c], note, scaled)
            mixed.append(rows_mixed)
        power = jnp.exp2(note[0, 0] - NOTE)
        return reduce_bonds(mixed, h_scale / z_scale), power, total

    reach = ENV * m**0.5
    spread_of = 9.0 * jnp.max(jnp.abs(entry_values)) + F32(1e-30)
    z_scale = F16_TOP / (1.02 * reach * spread_of)
    h_scale = F16_TOP / (8.4 * reach * reach * spread_of)
    small = F32(1e-18)

    squares = call(squares_kernel, [((8, 128), F32)], [], [psi])[0]
    psi_norm = jnp.sqrt(squares[0, 0]) + small
    piece, power, _ = hamiltonian(psi, squares, False)
    bound = F16_TOP / (1.05 * (power * (F16_TOP / h_scale) + 2.0 * psi_norm))
    piece = piece * (power * (bound / h_scale)) - (bound * recurrence[0]) * own_rows(psi)
    resid, squares = share_bonds(piece.astype(F16), 1.0 / bound)

    piece, power, tile = hamiltonian(resid, squares, True)
    own_norm = jnp.sqrt(squares[0, 0]) + small
    gain = 1.0 / jnp.sqrt(tile[0, 0] / cells + EPS)
    vec_one = resid * gain
    bound = gain * (power * (F16_TOP / h_scale) + 2.0 * own_norm) + 2.0 * psi_norm
    bound = F16_TOP / (1.05 * bound)
    piece = piece * (power * gain * (bound / h_scale))
    piece = piece - (bound * gain * recurrence[1]) * own_rows(resid)
    piece = piece - (bound * recurrence[2]) * own_rows(psi)
    resid, squares = share_bonds(piece.astype(F16), 1.0 / bound)
    mean = of_lines(of_line(squares))[0, 0] / cells
    vec_two = resid * (1.0 / jnp.sqrt(mean + EPS))
    return (vec_one[None], vec_two[None])


def solution(mesh):
    in_specs = (
        P("sector", None, None),
        P("mpo", "sector", None, None),
        P("mpo", "sector", None, None),
        P(),
        P(),
        P(),
        P(),
        P(),
    )
    out_specs = (P("sector", None, None), P("sector", None, None))
    return jax.shard_map(local, mesh=mesh, in_specs=in_specs, out_specs=out_specs, check_vma=False)
```

```python
import functools

import jax
import jax.numpy as jnp
from jax import lax
from jax.experimental import pallas as pl
from jax.experimental.pallas import tpu as pltpu
from jax.sharding import PartitionSpec as P

EPS = 1e-06
SIDE = 4
CHUNKS = 2
LATE = True
WHEN = 1
ENV = 0.21875
F16_TOP = 60000.0
TILE = 16
NOTE = 130.0
F32, BF16, F16 = jnp.float32, jnp.bfloat16, jnp.float16
VMEM_LIMIT = 16 * 1024 * 1024
in_vmem = pl.BlockSpec(memory_space=pltpu.VMEM)
in_smem = pl.BlockSpec(memory_space=pltpu.SMEM)


def along_x(block, step):
    route = [
        (SIDE * z + x, SIDE * z + (x + step) % SIDE) for z in range(SIDE) for x in range(SIDE)
    ]
    return lax.ppermute(block, "sector", route)


def along_z(block, step):
    count = SIDE * SIDE
    route = [(i, i + SIDE * step) for i in range(count) if 0 <= i + SIDE * step < count]
    return lax.ppermute(block, "sector", route)


def around_z(block, step):
    count = SIDE * SIDE
    return lax.ppermute(
        block, "sector", [(i, (i + SIDE * step) % count) for i in range(count)]
    )


def along_y(block, step):
    route = [
        (2 * y + core, 2 * ((y + step) % SIDE) + core) for y in range(SIDE) for core in range(2)
    ]
    return lax.ppermute(block, "mpo", route)


def other_core(block):
    return lax.ppermute(block, "mpo", [(i, i ^ 1) for i in range(2 * SIDE)])


def pick(array, index):
    return lax.dynamic_index_in_dim(array, index, 0, keepdims=False)


def after(value, earlier):
    return lax.optimization_barrier((value, earlier))[0]


def call(body, outs, smem, vmem, scratch=(), flops=0):
    shapes = [jax.ShapeDtypeStruct(shape, dtype) for shape, dtype in outs]
    moved = sum(a.size * a.dtype.itemsize for a in vmem)
    moved += sum(s.size * s.dtype.itemsize for s in shapes)
    return pl.pallas_call(
        body,
        out_shape=shapes,
        in_specs=[in_smem] * len(smem) + [in_vmem] * len(vmem),
        out_specs=[in_vmem] * len(outs),
        scratch_shapes=list(scratch),
        compiler_params=pltpu.CompilerParams(vmem_limit_bytes=VMEM_LIMIT),
        cost_estimate=pl.CostEstimate(flops=flops, bytes_accessed=moved, transcendentals=0),
    )(*smem, *vmem)


def halves_of(array):
    head = array.astype(BF16)
    return head, (array - head.astype(F32)).astype(BF16)


def dot(a, b):
    return jnp.dot(a, b, preferred_element_type=F32)


def product_kernel(row, noted, given, place, left, vector, *refs):
    if given:
        squares, *refs = refs
    outs, acc = refs[:SIDE], refs[-1]
    rows, m = acc.shape
    part = rows // SIDE
    left_head, left_tail = halves_of(left[pl.ds(row, rows), :])
    wide = m // 3
    total = jnp.zeros((8, wide), F32)
    for n in range(3):
        cols = slice(n * wide, (n + 1) * wide)
        value = vector[:, cols]
        if not given:
            total = total + jnp.sum((value * value).reshape(-1, 8, wide), axis=0)
        head, tail = halves_of(value)
        acc[:, cols] = dot(left_head, head) + (dot(left_head, tail) + dot(left_tail, head))
    x = place[0]
    if not given:
        squares = refs[SIDE]
        squares[...] = jnp.full(squares.shape, jnp.sum(total), F32)
    if noted:
        power = jnp.ceil(0.5 * jnp.log2(jnp.clip(squares[...], 1e-36, 1e36)) + 0.01)
        note = jnp.broadcast_to(power[:1, :1] + NOTE, (TILE, m)).astype(BF16)
    for d in range(SIDE):
        start = pl.multiple_of(lax.rem(x + d, SIDE) * part, part)
        outs[d][:part, :] = acc[pl.ds(start, part), :].astype(BF16)
        if noted:
            outs[d][part:, :] = note


def select_kernel(part, skips, *refs):
    near, outs = refs[:SIDE], refs[SIDE:]
    for skip, out in ((skips[0], outs[0]), (skips[1], outs[1])):
        for e in range(SIDE):
            at = jnp.where(skip < e, e - 1, min(e, SIDE - 2)) * part

            @pl.when(skip != e)
            def _():
                out[pl.ds(pl.multiple_of(at, part), part), :] = near[e][:part, :]

        if near[0].shape[0] > part:
            notes = [n[part:, :].astype(F32) for n in near]
            out[(SIDE - 1) * part :, :] = functools.reduce(jnp.maximum, notes).astype(BF16)


def mix_kernel(noted, weight, scale, *refs):
    near, up, down = refs[:SIDE], refs[SIDE], refs[SIDE + 1]
    if noted:
        out, note = refs[SIDE + 2 :]
        part = out.shape[1]
        notes = [n[part:, :].astype(F32) for n in near]
        notes += [n[(SIDE - 1) * part :, :].astype(F32) for n in (up, down)]
        note[...] = functools.reduce(jnp.maximum, notes)
    else:
        note, out = refs[SIDE + 2 :]
        part = out.shape[1]
    factor = jnp.exp2(NOTE - note[...]) * scale[0]

    def step(i, carry):
        def at(piece):
            return pl.ds(pl.multiple_of(piece * part + i * TILE, TILE), TILE)

        blocks = [near[j][at(0), :] for j in range(SIDE)]
        blocks += [up[at(j), :] for j in range(SIDE - 1)] + [down[at(j), :] for j in range(SIDE - 1)]
        sums = [None] * SIDE
        for j, block in enumerate(blocks):
            block = block.astype(F32)
            for d in range(SIDE):
                term = block * weight[d * 10 + j]
                sums[d] = term if j == 0 else sums[d] + term
        for d in range(SIDE):
            out[d, at(0), :] = sums[d] * factor
        return carry

    lax.fori_loop(0, part // TILE, step, 0)


def term_kernel(place, scale, mixed, right, mine, theirs, acc):
    eighth = mine.shape[1]
    half = SIDE * eighth
    left_head, left_tail = halves_of(mixed[...])
    wide = acc.shape[1] // 3
    for n in range(3):
        cols = slice(n * wide, (n + 1) * wide)
        head, tail = halves_of(right[:, cols])
        acc[:, cols] = dot(left_head, head) + (dot(left_head, tail) + dot(left_tail, head))
    y, core, factor = place[1], place[2], scale[0]
    for e in range(SIDE):
        quarter = lax.rem(y + e, SIDE) * eighth
        for out, side in ((mine, core), (theirs, 1 - core)):
            start = pl.multiple_of(side * half + quarter, eighth)
            out[e] = acc[pl.ds(start, eighth), :] * factor


def assemble_kernel(place, scale, mine, theirs, out, stats):
    chunks, eighth, m = mine.shape[1:]
    part = 2 * eighth
    x, y, core = place[0], place[1], place[2]
    squares = jnp.zeros((8, m), F32)
    for c in range(chunks):
        for block, side in ((mine, core), (theirs, 1 - core)):
            for e in range(SIDE):
                quarter = lax.rem(y - e + SIDE, SIDE)
                k = lax.rem(x - 2 * side - quarter // 2 + SIDE, SIDE)
                start = c * SIDE * part + k * part + lax.rem(quarter, 2) * eighth
                value = block[e, c] * scale[0]
                out[pl.ds(pl.multiple_of(start, eighth), eighth), :] = value
                squares = squares + jnp.sum((value * value).reshape(-1, 8, m), axis=0)
    stats[...] = jnp.full(stats.shape, jnp.sum(squares), F32)


def combined(tiles):
    return functools.reduce(jnp.add, tiles)


def of_line(tile):
    return combined([tile] + [along_x(tile, d) for d in range(1, SIDE)])


def of_lines(line):
    return combined([line] + [around_z(line, d) for d in range(1, SIDE)])


def local(
    psi, left_env, right_env, sector_label, charge_step, coef_index, entry_values, recurrence
):
    slot = lax.axis_index("sector")
    bond = lax.axis_index("mpo")
    z, x = slot // SIDE, slot % SIDE
    y, core = bond // 2, bond % 2
    place = jnp.stack([x, y, core]).astype(jnp.int32)
    psi, left, right = psi[0], left_env[0, 0], right_env[0, 0]
    m = psi.shape[0]
    slots = sector_label.shape[0]
    cells = float(slots * m * m)
    rows = m // CHUNKS
    part = rows // SIDE
    half = rows // 2
    eighth = half // SIDE
    flops = 6 * rows * m * m

    ds = jnp.arange(SIDE, dtype=jnp.int32)
    three = ds[: SIDE - 1]
    skip_up, skip_down = x, (x + 1) % SIDE
    skips = jnp.stack([skip_up, skip_down]).astype(jnp.int32)
    up_d = three + (three >= skip_up)
    down_d = three + (three >= skip_down)
    goal = SIDE * z + (x + ds) % SIDE
    source = jnp.concatenate(
        [
            SIDE * z + (x - ds) % SIDE,
            SIDE * (z - 1) + (x - up_d) % SIDE,
            SIDE * (z + 1) + (x - down_d) % SIDE,
        ]
    )

    table = jnp.arange(entry_values.shape[0], dtype=jnp.int32)
    every = jnp.arange(slots, dtype=jnp.int32)
    step_bond, index_bond = pick(charge_step, bond), pick(coef_index, bond)
    values = jnp.sum(jnp.where(index_bond[..., None] == table, entry_values, F32(0.0)), axis=-1)
    target = sector_label[:, None] + step_bond
    goal_label = jnp.sum(jnp.where(goal[:, None] == every, sector_label, 0), axis=1)
    into = jnp.sum(
        jnp.where(target[None] == goal_label[:, None, None], values[None], F32(0.0)), axis=2
    )
    weight = jnp.sum(
        jnp.where(source[None, :, None] == every, into[:, None, :], F32(0.0)), axis=2
    ).reshape(-1)

    def spread(pieces):
        return [pieces[0]] + [along_x(pieces[d], d) for d in range(1, SIDE)]

    def next_rows(near, earlier):
        noted = near[0].shape[0] > part
        out = (((SIDE - 1) * part + TILE * noted, m), BF16)
        up, down = call(functools.partial(select_kernel, part), [out] * 2, [skips], near)
        up, down = after((up, down), earlier)
        return [along_z(up, 1), along_z(down, -1)]

    def mix(near, beyond, note, weights):
        noted = near[0].shape[0] > part
        out, note_out = ((SIDE, part, m), F32), ((TILE, m), F32)
        got = call(
            functools.partial(mix_kernel, noted),
            [out] + [note_out] * noted,
            [weights, z_scale.reshape(1)],
            near + beyond + ([] if noted else [note]),
            flops=80 * part * m,
        )
        sums = got[0].astype(F16)
        mixed = jnp.concatenate([sums[0]] + [along_x(sums[d], d) for d in range(1, SIDE)])
        return mixed, got[1] if noted else note

    def reduce_bonds(mixed, scale):
        chips = []
        for c in range(CHUNKS):
            mine, theirs = call(
                term_kernel,
                [((SIDE, eighth, m), F32)] * 2,
                [place, scale.reshape(1)],
                [mixed[c].astype(F32), right],
                [pltpu.VMEM((rows, m), F32)],
                flops,
            )
            chips.append(mine + other_core(theirs.astype(F16)).astype(F32))
        chip = jnp.stack(chips, 1)
        sent = chip.astype(F16)
        total = chip[0]
        for e in range(1, SIDE):
            total = total + along_y(sent[e], e).astype(F32)
        return total

    def share_bonds(piece, factor):
        mine = jnp.stack([piece] + [along_y(piece, e) for e in range(1, SIDE)])
        return call(
            assemble_kernel,
            [((m, m), F32), ((8, 128), F32)],
            [place, factor.reshape(1)],
            [mine.astype(F32), other_core(mine).astype(F32)],
        )

    def own_rows(array):
        k = (x - 2 * core - y // 2) % SIDE
        start = k * part + (y % 2) * eighth
        return lax.dynamic_slice_in_dim(array.reshape(CHUNKS, rows, m), start, eighth, 1)

    def products(chunk, vector, squares):
        noted = chunk == 0
        given = squares is not None
        return call(
            functools.partial(product_kernel, chunk * rows, noted, given),
            [((part + TILE * noted, m), BF16)] * SIDE + [((8, 128), F32)] * (not given),
            [place],
            [left, vector] + [squares] * given,
            [pltpu.VMEM((rows, m), F32)],
            flops,
        )

    def hamiltonian(vector, squares, summed):
        pieces = [list(products(0, vector, squares))]
        if squares is None:
            squares = pieces[0].pop()
        pieces += [products(c, vector, squares) for c in range(1, CHUNKS)]
        near, beyond, mixed, note, total = [], [], [], None, squares
        for p in pieces:
            near.append(after(spread(after(p, near[-1:])), pieces[-1][0]))
        scaled = weight
        if summed:
            line = of_line(after(squares, pieces[-1][0]))
            if LATE:
                near[-1] = after(near[-1], line)
        for p in near:
            beyond.append(next_rows(p, beyond[-1:]))
        if summed:
            total = of_lines(line)
        for c in range(CHUNKS):
            if summed and c == WHEN:
                scaled = after(scaled, total)
            rows_mixed, note = mix(near[c], beyond[c], note, scaled)
            mixed.append(rows_mixed)
        power = jnp.exp2(note[0, 0] - NOTE)
        return reduce_bonds(mixed, h_scale / z_scale), power, total

    reach = ENV * m**0.5
    spread_of = 9.0 * jnp.max(jnp.abs(entry_values)) + F32(1e-30)
    z_scale = F16_TOP / (1.02 * reach * spread_of)
    h_scale = F16_TOP / (8.4 * reach * reach * spread_of)
    small = F32(1e-18)

    piece, power, squares = hamiltonian(psi, None, False)
    psi_norm = jnp.sqrt(squares[0, 0]) + small
    bound = F16_TOP / (1.05 * (power * (F16_TOP / h_scale) + 2.0 * psi_norm))
    piece = piece * (power * (bound / h_scale)) - (bound * recurrence[0]) * own_rows(psi)
    resid, squares = share_bonds(piece.astype(F16), 1.0 / bound)

    piece, power, tile = hamiltonian(resid, squares, True)
    own_norm = jnp.sqrt(squares[0, 0]) + small
    gain = 1.0 / jnp.sqrt(tile[0, 0] / cells + EPS)
    vec_one = resid * gain
    bound = gain * (power * (F16_TOP / h_scale) + 2.0 * own_norm) + 2.0 * psi_norm
    bound = F16_TOP / (1.05 * bound)
    piece = piece * (power * gain * (bound / h_scale))
    piece = piece - (bound * gain * recurrence[1]) * own_rows(resid)
    piece = piece - (bound * recurrence[2]) * own_rows(psi)
    resid, squares = share_bonds(piece.astype(F16), 1.0 / bound)
    mean = of_lines(of_line(squares))[0, 0] / cells
    vec_two = resid * (1.0 / jnp.sqrt(mean + EPS))
    return (vec_one[None], vec_two[None])


def solution(mesh):
    in_specs = (
        P("sector", None, None),
        P("mpo", "sector", None, None),
        P("mpo", "sector", None, None),
        P(),
        P(),
        P(),
        P(),
        P(),
    )
    out_specs = (P("sector", None, None), P("sector", None, None))
    return jax.shard_map(local, mesh=mesh, in_specs=in_specs, out_specs=out_specs, check_vma=False)
```

```python
import functools

import jax
import jax.numpy as jnp
from jax import lax
from jax.experimental import pallas as pl
from jax.experimental.pallas import tpu as pltpu
from jax.sharding import PartitionSpec as P

EPS = 1e-06
SIDE = 4
CHUNKS = 2
LATE = True
WHEN = 1
ENV = 0.21875
F16_TOP = 60000.0
TILE = 16
NOTE = 130.0
F32, BF16, F16 = jnp.float32, jnp.bfloat16, jnp.float16
VMEM_LIMIT = 16 * 1024 * 1024
in_vmem = pl.BlockSpec(memory_space=pltpu.VMEM)
in_smem = pl.BlockSpec(memory_space=pltpu.SMEM)


def along_x(block, step):
    route = [
        (SIDE * z + x, SIDE * z + (x + step) % SIDE) for z in range(SIDE) for x in range(SIDE)
    ]
    return lax.ppermute(block, "sector", route)


def along_z(block, step):
    count = SIDE * SIDE
    route = [(i, i + SIDE * step) for i in range(count) if 0 <= i + SIDE * step < count]
    return lax.ppermute(block, "sector", route)


def around_z(block, step):
    count = SIDE * SIDE
    return lax.ppermute(
        block, "sector", [(i, (i + SIDE * step) % count) for i in range(count)]
    )


def along_y(block, step):
    route = [
        (2 * y + core, 2 * ((y + step) % SIDE) + core) for y in range(SIDE) for core in range(2)
    ]
    return lax.ppermute(block, "mpo", route)


def other_core(block):
    return lax.ppermute(block, "mpo", [(i, i ^ 1) for i in range(2 * SIDE)])


def pick(array, index):
    return lax.dynamic_index_in_dim(array, index, 0, keepdims=False)


def after(value, earlier):
    return lax.optimization_barrier((value, earlier))[0]


def call(body, outs, smem, vmem, scratch=(), flops=0):
    shapes = [jax.ShapeDtypeStruct(shape, dtype) for shape, dtype in outs]
    moved = sum(a.size * a.dtype.itemsize for a in vmem)
    moved += sum(s.size * s.dtype.itemsize for s in shapes)
    return pl.pallas_call(
        body,
        out_shape=shapes,
        in_specs=[in_smem] * len(smem) + [in_vmem] * len(vmem),
        out_specs=[in_vmem] * len(outs),
        scratch_shapes=list(scratch),
        compiler_params=pltpu.CompilerParams(vmem_limit_bytes=VMEM_LIMIT),
        cost_estimate=pl.CostEstimate(flops=flops, bytes_accessed=moved, transcendentals=0),
    )(*smem, *vmem)


def halves_of(array):
    head = array.astype(BF16)
    return head, (array - head.astype(F32)).astype(BF16)


def dot(a, b):
    return jnp.dot(a, b, preferred_element_type=F32)


def product_kernel(row, noted, given, place, left, vector, *refs):
    if given:
        squares, *refs = refs
    outs, acc = refs[:SIDE], refs[-1]
    rows, m = acc.shape
    part = rows // SIDE
    left_head, left_tail = halves_of(left[pl.ds(row, rows), :])
    wide = m // 3
    total = jnp.zeros((8, wide), F32)
    for n in range(3):
        cols = slice(n * wide, (n + 1) * wide)
        value = vector[:, cols]
        if not given:
            total = total + jnp.sum((value * value).reshape(-1, 8, wide), axis=0)
        head, tail = halves_of(value)
        acc[:, cols] = dot(left_head, head) + (dot(left_head, tail) + dot(left_tail, head))
    x = place[0]
    if not given:
        squares = refs[SIDE]
        squares[...] = jnp.full(squares.shape, jnp.sum(total), F32)
    if noted:
        power = jnp.ceil(0.5 * jnp.log2(jnp.clip(squares[...], 1e-36, 1e36)) + 0.01)
        note = jnp.broadcast_to(power[:1, :1] + NOTE, (TILE, m)).astype(BF16)
    for d in range(SIDE):
        start = pl.multiple_of(lax.rem(x + d, SIDE) * part, part)
        outs[d][:part, :] = acc[pl.ds(start, part), :].astype(BF16)
        if noted:
            outs[d][part:, :] = note


def select_kernel(part, skips, *refs):
    near, outs = refs[:SIDE], refs[SIDE:]
    for skip, out in ((skips[0], outs[0]), (skips[1], outs[1])):
        for e in range(SIDE):
            at = jnp.where(skip < e, e - 1, min(e, SIDE - 2)) * part

            @pl.when(skip != e)
            def _():
                out[pl.ds(pl.multiple_of(at, part), part), :] = near[e][:part, :]

        if near[0].shape[0] > part:
            notes = [n[part:, :].astype(F32) for n in near]
            out[(SIDE - 1) * part :, :] = functools.reduce(jnp.maximum, notes).astype(BF16)


def mix_kernel(noted, weight, scale, *refs):
    near, up, down = refs[:SIDE], refs[SIDE], refs[SIDE + 1]
    if noted:
        out, note = refs[SIDE + 2 :]
        part = out.shape[1]
        notes = [n[part:, :].astype(F32) for n in near]
        notes += [n[(SIDE - 1) * part :, :].astype(F32) for n in (up, down)]
        note[...] = functools.reduce(jnp.maximum, notes)
    else:
        note, out = refs[SIDE + 2 :]
        part = out.shape[1]
    factor = jnp.exp2(NOTE - note[...]) * scale[0]

    def step(i, carry):
        def at(piece):
            return pl.ds(pl.multiple_of(piece * part + i * TILE, TILE), TILE)

        blocks = [near[j][at(0), :] for j in range(SIDE)]
        blocks += [up[at(j), :] for j in range(SIDE - 1)] + [down[at(j), :] for j in range(SIDE - 1)]
        sums = [None] * SIDE
        for j, block in enumerate(blocks):
            block = block.astype(F32)
            for d in range(SIDE):
                term = block * weight[d * 10 + j]
                sums[d] = term if j == 0 else sums[d] + term
        for d in range(SIDE):
            out[d, at(0), :] = sums[d] * factor
        return carry

    lax.fori_loop(0, part // TILE, step, 0)


def term_kernel(place, scale, mixed, right, mine, theirs, acc):
    eighth = mine.shape[1]
    half = SIDE * eighth
    left_head, left_tail = halves_of(mixed[...])
    wide = acc.shape[1] // 3
    for n in range(3):
        cols = slice(n * wide, (n + 1) * wide)
        head, tail = halves_of(right[:, cols])
        acc[:, cols] = dot(left_head, head) + (dot(left_head, tail) + dot(left_tail, head))
    y, core, factor = place[1], place[2], scale[0]
    for e in range(SIDE):
        quarter = lax.rem(y + e, SIDE) * eighth
        for out, side in ((mine, core), (theirs, 1 - core)):
            start = pl.multiple_of(side * half + quarter, eighth)
            out[e] = acc[pl.ds(start, eighth), :] * factor


def assemble_kernel(place, scale, mine, theirs, out, stats):
    chunks, eighth, m = mine.shape[1:]
    part = 2 * eighth
    x, y, core = place[0], place[1], place[2]
    squares = jnp.zeros((8, m), F32)
    for c in range(chunks):
        for block, side in ((mine, core), (theirs, 1 - core)):
            for e in range(SIDE):
                quarter = lax.rem(y - e + SIDE, SIDE)
                k = lax.rem(x - 2 * side - quarter // 2 + SIDE, SIDE)
                start = c * SIDE * part + k * part + lax.rem(quarter, 2) * eighth
                value = block[e, c] * scale[0]
                out[pl.ds(pl.multiple_of(start, eighth), eighth), :] = value
                squares = squares + jnp.sum((value * value).reshape(-1, 8, m), axis=0)
    stats[...] = jnp.full(stats.shape, jnp.sum(squares), F32)


def combined(tiles):
    return functools.reduce(jnp.add, tiles)


def of_line(tile):
    return combined([tile] + [along_x(tile, d) for d in range(1, SIDE)])


def of_lines(line):
    return combined([line] + [around_z(line, d) for d in range(1, SIDE)])


def local(
    psi, left_env, right_env, sector_label, charge_step, coef_index, entry_values, recurrence
):
    slot = lax.axis_index("sector")
    bond = lax.axis_index("mpo")
    z, x = slot // SIDE, slot % SIDE
    y, core = bond // 2, bond % 2
    place = jnp.stack([x, y, core]).astype(jnp.int32)
    psi, left, right = psi[0], left_env[0, 0], right_env[0, 0]
    m = psi.shape[0]
    slots = sector_label.shape[0]
    cells = float(slots * m * m)
    rows = m // CHUNKS
    part = rows // SIDE
    half = rows // 2
    eighth = half // SIDE
    flops = 6 * rows * m * m

    ds = jnp.arange(SIDE, dtype=jnp.int32)
    three = ds[: SIDE - 1]
    skip_up, skip_down = x, (x + 1) % SIDE
    skips = jnp.stack([skip_up, skip_down]).astype(jnp.int32)
    up_d = three + (three >= skip_up)
    down_d = three + (three >= skip_down)
    goal = SIDE * z + (x + ds) % SIDE
    source = jnp.concatenate(
        [
            SIDE * z + (x - ds) % SIDE,
            SIDE * (z - 1) + (x - up_d) % SIDE,
            SIDE * (z + 1) + (x - down_d) % SIDE,
        ]
    )

    table = jnp.arange(entry_values.shape[0], dtype=jnp.int32)
    every = jnp.arange(slots, dtype=jnp.int32)
    step_bond, index_bond = pick(charge_step, bond), pick(coef_index, bond)
    values = jnp.sum(jnp.where(index_bond[..., None] == table, entry_values, F32(0.0)), axis=-1)
    target = sector_label[:, None] + step_bond
    goal_label = jnp.sum(jnp.where(goal[:, None] == every, sector_label, 0), axis=1)
    into = jnp.sum(
        jnp.where(target[None] == goal_label[:, None, None], values[None], F32(0.0)), axis=2
    )
    weight = jnp.sum(
        jnp.where(source[None, :, None] == every, into[:, None, :], F32(0.0)), axis=2
    ).reshape(-1)

    def spread(pieces):
        return [pieces[0]] + [along_x(pieces[d], d) for d in range(1, SIDE)]

    def next_rows(near, earlier):
        noted = near[0].shape[0] > part
        out = (((SIDE - 1) * part + TILE * noted, m), BF16)
        up, down = call(functools.partial(select_kernel, part), [out] * 2, [skips], near)
        up, down = after((up, down), earlier)
        return [along_z(up, 1), along_z(down, -1)]

    def mix(near, beyond, note, weights):
        noted = near[0].shape[0] > part
        out, note_out = ((SIDE, part, m), F32), ((TILE, m), F32)
        got = call(
            functools.partial(mix_kernel, noted),
            [out] + [note_out] * noted,
            [weights, z_scale.reshape(1)],
            near + beyond + ([] if noted else [note]),
            flops=80 * part * m,
        )
        sums = got[0].astype(F16)
        mixed = jnp.concatenate([sums[0]] + [along_x(sums[d], d) for d in range(1, SIDE)])
        return mixed, got[1] if noted else note

    def reduce_bonds(mixed, scale):
        chips = []
        for c in range(CHUNKS):
            mine, theirs = call(
                term_kernel,
                [((SIDE, eighth, m), F32)] * 2,
                [place, scale.reshape(1)],
                [mixed[c].astype(F32), right],
                [pltpu.VMEM((rows, m), F32)],
                flops,
            )
            chips.append(mine + other_core(theirs.astype(F16)).astype(F32))
        chip = jnp.stack(chips, 1)
        sent = chip.astype(F16)
        total = chip[0]
        for e in range(1, SIDE):
            total = total + along_y(sent[e], e).astype(F32)
        return total

    def share_bonds(piece, factor):
        mine = jnp.stack([piece] + [along_y(piece, e) for e in range(1, SIDE)])
        return call(
            assemble_kernel,
            [((m, m), F32), ((8, 128), F32)],
            [place, factor.reshape(1)],
            [mine.astype(F32), other_core(mine).astype(F32)],
        )

    def own_rows(array):
        k = (x - 2 * core - y // 2) % SIDE
        start = k * part + (y % 2) * eighth
        return lax.dynamic_slice_in_dim(array.reshape(CHUNKS, rows, m), start, eighth, 1)

    def products(chunk, vector, squares):
        noted = chunk == 0
        given = squares is not None
        return call(
            functools.partial(product_kernel, chunk * rows, noted, given),
            [((part + TILE * noted, m), BF16)] * SIDE + [((8, 128), F32)] * (not given),
            [place],
            [left, vector] + [squares] * given,
            [pltpu.VMEM((rows, m), F32)],
            flops,
        )

    def hamiltonian(vector, squares, summed):
        pieces = [list(products(0, vector, squares))]
        if squares is None:
            squares = pieces[0].pop()
        pieces += [products(c, vector, squares) for c in range(1, CHUNKS)]
        near, beyond, mixed, note, total = [], [], [], None, squares
        for p in pieces:
            near.append(after(spread(after(p, near[-1:])), pieces[-1][0]))
        scaled = weight
        if summed:
            line = of_line(after(squares, pieces[-1][0]))
            if LATE:
                near[-1] = after(near[-1], line)
        for p in near:
            beyond.append(next_rows(p, beyond[-1:]))
        if summed:
            total = of_lines(line)
        for c in range(CHUNKS):
            if summed and c == WHEN:
                scaled = after(scaled, total)
            rows_mixed, note = mix(near[c], beyond[c], note, scaled)
            mixed.append(rows_mixed)
        power = jnp.exp2(note[0, 0] - NOTE)
        return reduce_bonds(mixed, h_scale / z_scale), power, total

    reach = ENV * m**0.5
    spread_of = 9.0 * jnp.max(jnp.abs(entry_values)) + F32(1e-30)
    z_scale = F16_TOP / (1.02 * reach * spread_of)
    h_scale = F16_TOP / (8.4 * reach * reach * spread_of)
    small = F32(1e-18)

    piece, power, squares = hamiltonian(psi, None, False)
    psi_norm = jnp.sqrt(squares[0, 0]) + small
    bound = F16_TOP / (1.05 * (power * (F16_TOP / h_scale) + 2.0 * psi_norm))
    piece = piece * (power * (bound / h_scale)) - (bound * recurrence[0]) * own_rows(psi)
    resid, squares = share_bonds(piece.astype(F16), 1.0 / bound)

    piece, power, tile = hamiltonian(resid, squares, True)
    own_norm = jnp.sqrt(squares[0, 0]) + small
    gain = 1.0 / jnp.sqrt(tile[0, 0] / cells + EPS)
    vec_one = resid * gain
    bound = gain * (power * (F16_TOP / h_scale) + 2.0 * own_norm) + 2.0 * psi_norm
    bound = F16_TOP / (1.05 * bound)
    piece = piece * (power * gain * (bound / h_scale))
    piece = piece - (bound * gain * recurrence[1]) * own_rows(resid)
    piece = piece - (bound * recurrence[2]) * own_rows(psi)
    piece = piece.astype(F16)
    own = jnp.sum(jnp.square(piece.astype(F32) * (1.0 / bound)))
    tile = of_lines(of_line(jnp.full((8, 128), own)))
    resid, _ = share_bonds(piece, 1.0 / bound)
    tile = combined([tile] + [along_y(tile, e) for e in range(1, SIDE)])
    mean = (tile + other_core(tile))[0, 0] / cells
    vec_two = resid * (1.0 / jnp.sqrt(mean + EPS))
    return (vec_one[None], vec_two[None])


def solution(mesh):
    in_specs = (
        P("sector", None, None),
        P("mpo", "sector", None, None),
        P("mpo", "sector", None, None),
        P(),
        P(),
        P(),
        P(),
        P(),
    )
    out_specs = (P("sector", None, None), P("sector", None, None))
    return jax.shard_map(local, mesh=mesh, in_specs=in_specs, out_specs=out_specs, check_vma=False)
```
